256 devices in a mesh: demo: 32 (over z, x), fsdp: 2 (over y_hi), sketch: 4 (over y_lo, core).
Axes of the slice: x: 4, y: 4 (y_hi: 2, y_lo: 2; y = y_hi * 2 + y_lo), z: 8, core: 2. Of those that a mesh axis runs over, the one named last changes fastest.
Arguments:
- activations: bfloat16 [128, 512, 8192], P('demo', 'sketch', 'fsdp'), may hold values from -6 to 6
- cotangents: bfloat16 [128, 512, 8192], P('demo', 'sketch', 'fsdp'), may hold values from -6 to 6
- lengths: int32 [128], P('demo'), may hold values from 64 to 512, as said below
- lowrank_contract_matrix: bfloat16 [8192, 128], P('fsdp', 'demo'), may hold values from -0.0625 to 0.0625
- lowrank_expand_matrix: bfloat16 [8192, 128], P('fsdp', 'demo'), may hold values from -0.0625 to 0.0625
- input_feature_sketch: bfloat16 [8192, 64], P('fsdp', 'demo'), may hold values from -0.0625 to 0.0625
- latent_random_map_contracting: bfloat16 [128, 128], replicated, may hold values from -0.5 to 0.5
- latent_random_map_expanding: bfloat16 [128, 64], replicated, may hold values from -0.5 to 0.5
- output_feature_sketch: bfloat16 [8192, 128], P('fsdp', 'demo'), may hold values from -0.0625 to 0.0625
- queries: bfloat16 [4096, 8192], P('demo', 'sketch'), may hold values from -6 to 6
Outputs:
- scores: float32 [128, 4096], P('sketch', 'demo')
The draws below stay inside these ranges and needn't reach their ends.
Inputs may be any that keep to these rules, and one draw needn't show every extreme that they name: `lengths`: positions from a demonstration's length on are padding; at least one demonstration uses all 512 positions.
All inputs are finite; a program needn't handle non-finite values.
Results may differ from the reference program's by a relative error of at most 0.0057.
Values may be sent and summed in bfloat16 or wider, within the bound.
No kernel may reach another device: no remote copies, remote signals or barrier semaphores. Data moves between devices by JAX's collectives and lax.ppermute only.
A program may use at most 64 MiB of HBM per device.

```python
import math
import jax
import jax.numpy as jnp
from jax import lax

HIDDEN_EMBED_DIM = 8192
QUERY_PROJ_DIM = 8192
LATENT_INNER_DIM = 128
PROBE_ROWS = 64
PROBE_COLUMNS = 128
K = 8192
LEN = 512
DEMOS = 128
NQ = 4096


def draw_lengths(key, part):
    key = jax.random.fold_in(key, 5)
    first, second = jax.random.split(key)
    values = jax.random.randint(first, (DEMOS,), LEN // 8, LEN + 1, dtype=jnp.int32)
    longest = jax.random.randint(second, (), 0, DEMOS, dtype=jnp.int32)
    return jnp.where(jnp.arange(DEMOS, dtype=jnp.int32) == longest, jnp.int32(LEN), values)


def block_scale(rng, shape, cuts, low, top_value):
    def one(axis_at, blocks):
        steps = jax.random.uniform(jax.random.fold_in(jax.random.fold_in(rng, 6), axis_at), (blocks,), jnp.float32, low / len(cuts), top_value / len(cuts))
        return jnp.repeat(jnp.exp(steps), shape[axis_at] // blocks).reshape((-1,) + (1,) * (len(shape) - axis_at - 1))

    factor_of = one(*cuts[0])
    for cut in cuts[1:]:
        factor_of = factor_of * one(*cut)
    return factor_of


def centred(own_key, dims, width, bound, cuts=(), kind=jnp.bfloat16):
    level = block_scale(own_key, dims, cuts, -0.22, 0.18) if cuts else 1.0
    array = jax.random.normal(own_key, dims, jnp.float32) * width * level
    return jnp.minimum(jnp.maximum(array, -bound), bound).astype(kind)


def setup_inputs(seed: int = 0) -> dict:
    seeds = jax.random.split(jax.random.key(seed), 11)
    return {
        "activations": centred(seeds[0], (DEMOS, LEN, HIDDEN_EMBED_DIM), 1.0, 6.0, ((0, 32), (1, 4), (2, 2))),
        "cotangents": centred(seeds[1], (DEMOS, LEN, QUERY_PROJ_DIM), 1.0, 6.0, ((0, 32), (1, 4), (2, 2))),
        "lengths": draw_lengths(jax.random.fold_in(seeds[10], 71), 0),
        "lowrank_contract_matrix": centred(seeds[3], (HIDDEN_EMBED_DIM, LATENT_INNER_DIM), HIDDEN_EMBED_DIM ** -0.5, 0.0625, ((0, 2), (1, 32))),
        "lowrank_expand_matrix": centred(seeds[4], (QUERY_PROJ_DIM, LATENT_INNER_DIM), QUERY_PROJ_DIM ** -0.5, 0.0625, ((0, 2), (1, 32))),
        "input_feature_sketch": centred(seeds[5], (HIDDEN_EMBED_DIM, PROBE_ROWS), HIDDEN_EMBED_DIM ** -0.5, 0.0625, ((0, 2), (1, 32))),
        "latent_random_map_contracting": centred(seeds[6], (LATENT_INNER_DIM, PROBE_COLUMNS), LATENT_INNER_DIM ** -0.5, 0.5),
        "latent_random_map_expanding": centred(seeds[7], (LATENT_INNER_DIM, PROBE_ROWS), LATENT_INNER_DIM ** -0.5, 0.5),
        "output_feature_sketch": centred(seeds[8], (QUERY_PROJ_DIM, PROBE_COLUMNS), QUERY_PROJ_DIM ** -0.5, 0.0625, ((0, 2), (1, 32))),
        "queries": centred(seeds[9], (NQ, K), 1.0, 6.0, ((0, 32), (1, 4))),
    }


def reference(activations, cotangents, lengths, lowrank_contract_matrix, lowrank_expand_matrix, input_feature_sketch, latent_random_map_contracting, latent_random_map_expanding, output_feature_sketch, queries):
    reduced_left_factor = jnp.dot(lowrank_contract_matrix, latent_random_map_expanding, preferred_element_type=jnp.float32).astype(jnp.bfloat16)
    left_map = jnp.concatenate([input_feature_sketch, reduced_left_factor], axis=1)
    reduced_right_factor = jnp.dot(lowrank_expand_matrix, latent_random_map_contracting, preferred_element_type=jnp.float32).astype(jnp.bfloat16)
    right_map = jnp.concatenate([reduced_right_factor, output_feature_sketch], axis=1)
    positions = jnp.arange(LEN, dtype=jnp.int32)
    padding = (positions[None, :] < lengths[:, None]).astype(jnp.float32)
    left_rows = jnp.dot(activations.reshape(DEMOS * LEN, HIDDEN_EMBED_DIM), left_map, preferred_element_type=jnp.float32)
    left_rows = left_rows.astype(jnp.bfloat16).reshape(DEMOS, LEN, 2, PROBE_ROWS)
    right_rows = jnp.dot(cotangents.reshape(DEMOS * LEN, QUERY_PROJ_DIM), right_map, preferred_element_type=jnp.float32)
    right_rows = (right_rows.reshape(DEMOS, LEN, 2 * PROBE_COLUMNS) * padding[:, :, None]).astype(jnp.bfloat16)
    right_rows = right_rows.reshape(DEMOS, LEN, 2, PROBE_COLUMNS)
    summed = jnp.einsum('ntpa,ntpb->nab', left_rows.astype(jnp.float32), right_rows.astype(jnp.float32), precision=lax.Precision.HIGHEST)
    demo_sketch = summed.reshape(DEMOS, K).astype(jnp.bfloat16)
    sketch_f = demo_sketch.astype(jnp.float32)
    query_f = queries.astype(jnp.float32)
    inner = jnp.dot(sketch_f, query_f.T, precision=lax.Precision.HIGHEST)
    demo_norm = jnp.sqrt(lax.optimization_barrier(jnp.sum(sketch_f * sketch_f, axis=1)) + 1e-06)
    query_norm = jnp.sqrt(lax.optimization_barrier(jnp.sum(query_f * query_f, axis=1)) + 1e-06)
    return math.sqrt(K) * inner / (demo_norm[:, None] * query_norm[None, :])
```

```python
import math

import jax
import jax.numpy as jnp
from jax import lax
from jax.sharding import PartitionSpec as P

PROBE_ROWS = 64
PROBE_COLUMNS = 128
RANK = 128
K = 8192
AXES = ("demo", "fsdp", "sketch")
Z, X, F, S = 8, 4, 2, 4
ROWS = 16


def pairs(step):
    out = []
    for z in range(Z):
        for x in range(X):
            for f in range(F):
                for s in range(S):
                    z2, x2, f2, s2 = step(z, x, f, s)
                    source = ((z * X + x) * F + f) * S + s
                    target = (((z2 % Z) * X + x2 % X) * F + f2) * S + s2
                    out.append((source, target))
    return out


CORE = pairs(lambda z, x, f, s: (z, x, f, s ^ 1))
NEAR = pairs(lambda z, x, f, s: (z, x, f, s ^ 2))
FAR = pairs(lambda z, x, f, s: (z, x, f ^ 1, s))
FAR_NEAR = pairs(lambda z, x, f, s: (z, x, f ^ 1, s ^ 2))


def shift(dz, dx):
    return pairs(lambda z, x, f, s: (z + dz, x + dx, f, s))


def send(value, moves):
    return lax.ppermute(value, AXES, moves)


def pick(value, index):
    return lax.dynamic_index_in_dim(value, index, 0, keepdims=False)


def map_weights(contracting, expanding, z, x):
    weights = jnp.zeros((2 * PROBE_ROWS + 2 * PROBE_COLUMNS, Z * X, ROWS), jnp.bfloat16)
    weights = weights.at[PROBE_ROWS : 2 * PROBE_ROWS, :, 0:4].set(
        expanding.T.reshape(PROBE_ROWS, Z * X, 4)
    )
    weights = weights.at[2 * PROBE_ROWS : 2 * PROBE_ROWS + PROBE_COLUMNS, :, 4:8].set(
        contracting.T.reshape(PROBE_COLUMNS, Z * X, 4)
    )
    weights = weights.at[2 * PROBE_ROWS + PROBE_COLUMNS :, :, 8:12].set(
        jnp.eye(PROBE_COLUMNS, dtype=jnp.bfloat16).reshape(PROBE_COLUMNS, Z * X, 4)
    )
    weights = weights.at[:PROBE_ROWS, :, 12:14].set(
        jnp.eye(PROBE_ROWS, dtype=jnp.bfloat16).reshape(PROBE_ROWS, Z * X, 2)
    )
    weights = weights.reshape(-1, Z, X, ROWS)
    z_order = (z - jnp.arange(Z)) % Z
    x_order = (x - jnp.arange(X)) % X
    weights = jnp.take(jnp.take(weights, z_order, axis=1), x_order, axis=2)
    return weights.reshape(-1, Z * X * ROWS)


def gather_x(block):
    return jnp.stack([block] + [send(block, shift(0, k)) for k in range(1, X)])


def gather_z(block):
    got = {0: block}
    up = down = block
    for k in range(1, Z // 2 + 1):
        up = send(up, shift(1, 0))
        got[k] = up
        if k < Z // 2:
            down = send(down, shift(-1, 0))
            got[Z - k] = down
    return jnp.stack([got[k] for k in range(Z)])


def shards(
    activations,
    cotangents,
    lengths,
    lowrank_contract_matrix,
    lowrank_expand_matrix,
    input_feature_sketch,
    latent_random_map_contracting,
    latent_random_map_expanding,
    output_feature_sketch,
    queries,
):
    demo_count, tok_local, feat = activations.shape
    demo = lax.axis_index("demo")
    z, x = demo // X, demo % X
    f = lax.axis_index("fsdp")
    s = lax.axis_index("sketch")
    near, core = s // 2, s % 2

    block = jnp.concatenate(
        [
            lowrank_contract_matrix.T,
            lowrank_expand_matrix.T,
            output_feature_sketch.T,
            input_feature_sketch.T,
            jnp.zeros((2, feat), jnp.bfloat16),
        ],
        axis=0,
    )
    half = feat // 2
    block = lax.dynamic_slice_in_dim(block, core * half, half, axis=1)
    rows = gather_z(gather_x(block)).reshape(Z * X * ROWS, half)
    other = send(rows, CORE)
    first = jnp.where(core == 0, rows, other)
    second = jnp.where(core == 0, other, rows)
    weights = map_weights(
        latent_random_map_contracting, latent_random_map_expanding, z, x
    )
    maps = jnp.concatenate(
        [
            jnp.dot(weights, first, preferred_element_type=jnp.float32).astype(jnp.bfloat16),
            jnp.dot(weights, second, preferred_element_type=jnp.float32).astype(jnp.bfloat16),
        ],
        axis=1,
    )
    tok_rows = demo_count * tok_local
    contract_last = (((1,), (1,)), ((), ()))
    right = lax.dot_general(
        cotangents.reshape(tok_rows, feat),
        maps[2 * PROBE_ROWS :],
        contract_last,
        preferred_element_type=jnp.float32,
    ).reshape(F, demo_count // F, tok_local, 2 * PROBE_COLUMNS)
    left = lax.dot_general(
        activations.reshape(tok_rows, feat),
        maps[: 2 * PROBE_ROWS],
        contract_last,
        preferred_element_type=jnp.float32,
    ).reshape(F, demo_count // F, tok_local, 2 * PROBE_ROWS)

    right_sum = pick(right, f) + send(pick(right, 1 - f), FAR)
    left_sum = pick(left, f) + send(pick(left, 1 - f), FAR)
    positions = s * tok_local + jnp.arange(tok_local, dtype=jnp.int32)
    own_lengths = pick(lengths.reshape(F, demo_count // F), f)
    padding = (positions[None, :] < own_lengths[:, None]).astype(jnp.float32)
    right_sum = right_sum * padding[:, :, None]
    own = demo_count // F
    left_rows = left_sum.astype(jnp.bfloat16).reshape(own, tok_local, 2, PROBE_ROWS)
    right_rows = right_sum.astype(jnp.bfloat16).reshape(own, tok_local, 2, PROBE_COLUMNS)
    partial_value = jnp.einsum(
        "ntpa,ntpb->nab", left_rows, right_rows, preferred_element_type=jnp.float32
    )
    parts = partial_value.reshape(own, 2, 2, K // S).transpose(2, 1, 0, 3)
    parts = pick(parts, core) + send(pick(parts, 1 - core), CORE)
    part = pick(parts, near) + send(pick(parts, 1 - near), NEAR)
    demo_sketch = part.astype(jnp.bfloat16)

    every_demo = gather_z(gather_x(demo_sketch)).reshape(Z * X * own, K // S)
    inner = lax.dot_general(
        every_demo, queries, contract_last, preferred_element_type=jnp.float32
    )
    every_f = every_demo.astype(jnp.float32)
    demo_squares = jnp.sum(every_f * every_f, axis=1, keepdims=True)
    query_f = queries.astype(jnp.float32)
    query_squares = jnp.sum(query_f * query_f, axis=1)[None, :]
    query_squares = query_squares + send(query_squares, CORE)
    query_squares = query_squares + send(query_squares, NEAR)
    nq = queries.shape[0]
    both = jnp.concatenate([inner, jnp.broadcast_to(demo_squares, inner.shape)], axis=1)
    both = both.reshape(Z, X, own, 2 * nq)
    z_order = (z - jnp.arange(Z)) % Z
    x_order = (x - jnp.arange(X)) % X
    both = jnp.take(jnp.take(both, z_order, axis=0), x_order, axis=1)
    both = both.reshape(2, 2, (Z // S) * X * own, 2 * nq).transpose(1, 0, 2, 3)
    pair = pick(both, core) + send(pick(both, 1 - core), CORE)
    mine, theirs = pick(pair, near), pick(pair, 1 - near)
    here = mine + send(theirs, NEAR)
    there = send(mine, FAR) + send(theirs, FAR_NEAR)
    total = jnp.stack([jnp.where(f == 0, here, there), jnp.where(f == 0, there, here)])
    total = total.reshape(F, (Z // S) * X, own, 2 * nq).transpose(1, 0, 2, 3).reshape(-1, 2 * nq)
    demo_norm = jnp.sqrt(total[:, nq:] + 1e-06)
    query_norm = jnp.sqrt(query_squares + 1e-06)
    return math.sqrt(K) * total[:, :nq] / (demo_norm * query_norm)


def solution(mesh):
    placed = (
        P("demo", "sketch", "fsdp"),
        P("demo", "sketch", "fsdp"),
        P("demo"),
        P("fsdp", "demo"),
        P("fsdp", "demo"),
        P("fsdp", "demo"),
        P(),
        P(),
        P("fsdp", "demo"),
        P("demo", "sketch"),
    )
    return jax.shard_map(
        shards, mesh=mesh, in_specs=placed, out_specs=P("sketch", "demo"), check_vma=False
    )
```

```python
import math

import jax
import jax.numpy as jnp
from jax import lax
from jax.experimental import pallas as pl
from jax.experimental.pallas import tpu as pltpu
from jax.sharding import PartitionSpec as P

PROBE_ROWS = 64
PROBE_COLUMNS = 128
K = 8192
AXES = ("demo", "fsdp", "sketch")
Z, X, F, S = 8, 4, 2, 4
ROWS = 16
LEFT = 2 * PROBE_ROWS
RIGHT = 2 * PROBE_COLUMNS
CHUNK = 512
FIRST = ((0,), (0,))
LAST = ((1,), (1,))


def pairs(step):
    out = []
    for z in range(Z):
        for x in range(X):
            for f in range(F):
                for s in range(S):
                    z2, x2, f2, s2 = step(z, x, f, s)
                    source = ((z * X + x) * F + f) * S + s
                    target = (((z2 % Z) * X + x2 % X) * F + f2) * S + s2
                    out.append((source, target))
    return out


CORE = pairs(lambda z, x, f, s: (z, x, f, s ^ 1))
NEAR = pairs(lambda z, x, f, s: (z, x, f, s ^ 2))
CORE_NEAR = pairs(lambda z, x, f, s: (z, x, f, s ^ 3))
FAR = pairs(lambda z, x, f, s: (z, x, f ^ 1, s))
FAR_NEAR = pairs(lambda z, x, f, s: (z, x, f ^ 1, s ^ 2))


def shift(dz, dx):
    return pairs(lambda z, x, f, s: (z + dz, x + dx, f, s))


def send(value, moves):
    return lax.ppermute(value, AXES, moves)


def dot(a, b, contract):
    return lax.dot_general(a, b, (contract, ((), ())), preferred_element_type=jnp.float32)


def cost(flops, moved):
    return pl.CostEstimate(flops=flops, bytes_accessed=moved, transcendentals=0)


def shape(dims, kind=jnp.float32):
    return jax.ShapeDtypeStruct(dims, kind)


def weights_kernel(order_ref, contracting_ref, expanding_ref, queries_ref, weights_ref, squares_ref):
    columns = Z * X * ROWS
    place = order_ref[...]
    kind = lax.broadcasted_iota(jnp.int32, (1, columns), 1) % ROWS

    def chosen(count, width, start):
        inside = (kind >= start) & (kind < start + width)
        target = jnp.where(inside, place * width + kind - start, -1)
        hit = lax.broadcasted_iota(jnp.int32, (count, columns), 0) == target
        return jnp.where(hit, 1.0, 0.0).astype(jnp.bfloat16)

    weights_ref[0:PROBE_ROWS] = chosen(PROBE_ROWS, 2, 12)
    weights_ref[PROBE_ROWS:LEFT] = dot(expanding_ref[...], chosen(128, 4, 0), FIRST).astype(
        jnp.bfloat16
    )
    weights_ref[LEFT : LEFT + PROBE_COLUMNS] = dot(
        contracting_ref[...], chosen(128, 4, 4), FIRST
    ).astype(jnp.bfloat16)
    weights_ref[LEFT + PROBE_COLUMNS :] = chosen(PROBE_COLUMNS, 4, 8)
    values = queries_ref[...].astype(jnp.float32)
    squares = jnp.sum(values * values, axis=1, keepdims=True)
    squares_ref[...] = jnp.broadcast_to(squares, (128, 128)).T[0:8]


def maps_kernel(weights_ref, *refs):
    rows = jnp.concatenate([ref[...] for ref in refs[:-1]], axis=0)
    refs[-1][...] = dot(weights_ref[...], rows, ((1,), (0,))).astype(jnp.bfloat16)


def own_kernel(info_ref, act_ref, cot_ref, maps_ref, left_ref, right_ref):
    left = dot(act_ref[...], maps_ref[0:LEFT], LAST)
    right = dot(cot_ref[...], maps_ref[LEFT:], LAST)

    @pl.when(pl.program_id(0) == 0)
    def _():
        left_ref[...] = left
        right_ref[...] = right

    @pl.when(pl.program_id(0) > 0)
    def _():
        left_ref[...] += left
        right_ref[...] += right


def other_kernel(info_ref, tokens_ref, maps_ref, part_ref, keep_ref, give_ref, total_ref):
    value = dot(tokens_ref[...], maps_ref[...], LAST)
    step = pl.program_id(0)

    @pl.when(step == 0)
    def _():
        total_ref[...] = part_ref[...] + value

    @pl.when(step > 0)
    def _():
        total_ref[...] += value

    @pl.when(step == pl.num_programs(0) - 1)
    def _():
        half = total_ref.shape[0] // F
        f = info_ref[1]
        keep_ref[...] = total_ref[pl.ds(pl.multiple_of(f * half, half), half)]
        give_ref[...] = total_ref[pl.ds(pl.multiple_of((1 - f) * half, half), half)]


def outer_kernel(
    info_ref, keep_left, got_left, keep_right, got_right, own_ref, core_ref, near_ref, both_ref, total_ref
):
    demos = total_ref.shape[0]
    tokens = keep_left.shape[0] // demos
    s = info_ref[2]
    position = s * tokens + lax.broadcasted_iota(jnp.int32, (tokens, 1), 0)
    for j in range(demos):
        at = slice(j * tokens, (j + 1) * tokens)
        padding = jnp.where(position < info_ref[3 + j], 1.0, 0.0)
        left = (keep_left[at] + got_left[at]).astype(jnp.bfloat16)
        right = ((keep_right[at] + got_right[at]) * padding).astype(jnp.bfloat16)
        total_ref[j] = dot(left[:, :PROBE_ROWS], right[:, :PROBE_COLUMNS], FIRST) + dot(
            left[:, PROBE_ROWS:], right[:, PROBE_COLUMNS:], FIRST
        )
    rows = PROBE_ROWS // S
    for k, ref in enumerate((own_ref, core_ref, near_ref, both_ref)):
        start = pl.multiple_of((s ^ k) * rows, rows)
        for j in range(demos):
            ref[j] = total_ref[j, pl.ds(start, rows)]


def inner_kernel(info_ref, demos_ref, queries_ref, squares_ref, keep_ref, give_ref, total_ref):
    sketches = demos_ref[...]
    nq = queries_ref.shape[0]
    values = sketches.astype(jnp.float32)
    total_ref[:, :nq] = dot(sketches, queries_ref[...], LAST)
    total_ref[:, nq:] = jnp.broadcast_to(
        jnp.sum(values * values, axis=1, keepdims=True), (sketches.shape[0], nq)
    )
    s = info_ref[2]
    rows = sketches.shape[0] // S
    for ref, at, k in ((keep_ref, 0, 0), (keep_ref, 1, 2), (give_ref, 0, 1), (give_ref, 1, 3)):
        start = pl.multiple_of((s ^ k) * rows, rows)
        ref[at, 0:rows] = total_ref[pl.ds(start, rows)]
        ref[at, rows:, :nq] = squares_ref[...]
        ref[at, rows:, nq:] = squares_ref[...]


def whole(count):
    return [pl.BlockSpec(memory_space=pltpu.VMEM)] * count


def gather_z(block):
    got = {0: block}
    up = down = block
    for k in range(1, Z // 2 + 1):
        up = send(up, shift(1, 0))
        got[k] = up
        if k < Z // 2:
            down = send(down, shift(-1, 0))
            got[Z - k] = down
    return [got[k] for k in range(Z)]


def shards(
    activations,
    cotangents,
    lengths,
    lowrank_contract_matrix,
    lowrank_expand_matrix,
    input_feature_sketch,
    latent_random_map_contracting,
    latent_random_map_expanding,
    output_feature_sketch,
    queries,
):
    demo_count, tok_local, feat = activations.shape
    own = demo_count // F
    tokens = demo_count * tok_local
    half = feat // 2
    steps = half // CHUNK
    nq = queries.shape[0]
    demo = lax.axis_index("demo")
    z, x = demo // X, demo % X
    f = lax.axis_index("fsdp")
    s = lax.axis_index("sketch")
    core = s % 2
    own_lengths = lax.dynamic_slice_in_dim(lengths, f * own, own)
    info = jnp.concatenate([jnp.stack([core, f, s]).astype(jnp.int32), own_lengths])
    z_order = (z - jnp.arange(Z)) % Z
    x_order = (x - jnp.arange(X)) % X
    order = jnp.repeat((z_order[:, None] * X + x_order[None, :]).reshape(-1), ROWS)[None, :]

    block = jnp.concatenate(
        [
            lowrank_contract_matrix.T,
            lowrank_expand_matrix.T,
            output_feature_sketch.T,
            input_feature_sketch.T,
            jnp.zeros((2, feat), jnp.bfloat16),
        ],
        axis=0,
    )
    block = lax.dynamic_slice_in_dim(block, core * half, half, axis=1)
    weights, query_squares = pl.pallas_call(
        weights_kernel,
        out_shape=[shape((LEFT + RIGHT, Z * X * ROWS), jnp.bfloat16), shape((8, 128))],
        in_specs=whole(4),
        out_specs=whole(2),
        cost_estimate=cost(10**8, 10**6),
    )(
        order.astype(jnp.int32),
        latent_random_map_contracting,
        latent_random_map_expanding,
        queries,
    )
    line = jnp.concatenate([block] + [send(block, shift(0, k)) for k in range(1, X)])
    line, weights, query_squares = lax.optimization_barrier((line, weights, query_squares))
    arrived = gather_z(line)
    maps = pl.pallas_call(
        maps_kernel,
        grid=(steps,),
        out_shape=shape((LEFT + RIGHT, half), jnp.bfloat16),
        in_specs=[pl.BlockSpec((LEFT + RIGHT, Z * X * ROWS), lambda j: (0, 0))]
        + [pl.BlockSpec((X * ROWS, CHUNK), lambda j: (0, j))] * Z,
        out_specs=pl.BlockSpec((LEFT + RIGHT, CHUNK), lambda j: (0, j)),
        cost_estimate=cost(2 * 384 * 512 * 2048, 4 * 10**6),
    )(weights, *arrived)
    other_maps = send(maps, CORE)

    act = activations.reshape(tokens, feat)
    cot = cotangents.reshape(tokens, feat)
    left_part, right_part = pl.pallas_call(
        own_kernel,
        out_shape=[shape((tokens, LEFT)), shape((tokens, RIGHT))],
        grid_spec=pltpu.PrefetchScalarGridSpec(
            num_scalar_prefetch=1,
            grid=(steps,),
            in_specs=[
                pl.BlockSpec((tokens, CHUNK), lambda j, info: (0, info[0] * steps + j)),
                pl.BlockSpec((tokens, CHUNK), lambda j, info: (0, info[0] * steps + j)),
                pl.BlockSpec((LEFT + RIGHT, CHUNK), lambda j, info: (0, j)),
            ],
            out_specs=[
                pl.BlockSpec((tokens, LEFT), lambda j, info: (0, 0)),
                pl.BlockSpec((tokens, RIGHT), lambda j, info: (0, 0)),
            ],
        ),
        cost_estimate=cost(2 * 512 * 384 * 2048, 6 * 10**6),
    )(info, act, cot, maps)

    def other_half(values, part, first, width):
        return pl.pallas_call(
            other_kernel,
            out_shape=[shape((tokens // F, width))] * 2,
            grid_spec=pltpu.PrefetchScalarGridSpec(
                num_scalar_prefetch=1,
                grid=(steps,),
                in_specs=[
                    pl.BlockSpec((tokens, CHUNK), lambda j, info: (0, (1 - info[0]) * steps + j)),
                    pl.BlockSpec(
                        (pl.Element(width), pl.Element(CHUNK)), lambda j, info: (first, j * CHUNK)
                    ),
                    pl.BlockSpec((tokens, width), lambda j, info: (0, 0)),
                ],
                out_specs=[pl.BlockSpec((tokens // F, width), lambda j, info: (0, 0))] * 2,
                scratch_shapes=[pltpu.VMEM((tokens, width), jnp.float32)],
            ),
            cost_estimate=cost(2 * 512 * width * 2048, 4 * 10**6),
        )(info, values, other_maps, part)

    keep_right, give_right = other_half(cot, right_part, LEFT, RIGHT)
    got_right = send(give_right, FAR)
    keep_left, give_left = other_half(act, left_part, 0, LEFT)
    got_left = send(give_left, FAR)

    rows = PROBE_ROWS // S
    mine, to_core, to_near, to_both = pl.pallas_call(
        outer_kernel,
        out_shape=[shape((own, rows, PROBE_COLUMNS))] * 4,
        in_specs=[pl.BlockSpec(memory_space=pltpu.SMEM)] + whole(4),
        out_specs=whole(4),
        scratch_shapes=[pltpu.VMEM((own, PROBE_ROWS, PROBE_COLUMNS), jnp.float32)],
        cost_estimate=cost(2 * 10**7, 10**6),
    )(info, keep_left, got_left, keep_right, got_right)
    summed = (mine + send(to_core, CORE)) + (send(to_near, NEAR) + send(to_both, CORE_NEAR))
    demo_sketch = summed.astype(jnp.bfloat16).reshape(own, K // S)

    copies = jnp.broadcast_to(demo_sketch[None], (Z * X, own, K // S))
    every_demo = lax.all_to_all(copies, "demo", 0, 0).reshape(Z * X * own, K // S)
    block_rows = Z * X * own // S
    keep, give = pl.pallas_call(
        inner_kernel,
        out_shape=[shape((2, block_rows + 8, 2 * nq))] * 2,
        in_specs=[pl.BlockSpec(memory_space=pltpu.SMEM)] + whole(3),
        out_specs=whole(2),
        scratch_shapes=[pltpu.VMEM((Z * X * own, 2 * nq), jnp.float32)],
        cost_estimate=cost(4 * 10**7, 10**6),
    )(info, every_demo, queries, query_squares)
    pair = keep + send(give, CORE)
    here = pair[0] + send(pair[1], NEAR)
    there = send(pair[0], FAR) + send(pair[1], FAR_NEAR)
    query_squares = here[block_rows : block_rows + 1, :nq]
    here, there = here[:block_rows], there[:block_rows]
    total = jnp.stack([jnp.where(f == 0, here, there), jnp.where(f == 0, there, here)])
    total = total.reshape(F, block_rows // own, own, 2 * nq).transpose(1, 0, 2, 3)
    total = total.reshape(F * block_rows, 2 * nq)
    demo_norm = jnp.sqrt(total[:, nq:] + 1e-06)
    query_norm = jnp.sqrt(query_squares + 1e-06)
    return math.sqrt(K) * total[:, :nq] / (demo_norm * query_norm)


def solution(mesh):
    placed = (
        P("demo", "sketch", "fsdp"),
        P("demo", "sketch", "fsdp"),
        P("demo"),
        P("fsdp", "demo"),
        P("fsdp", "demo"),
        P("fsdp", "demo"),
        P(),
        P(),
        P("fsdp", "demo"),
        P("demo", "sketch"),
    )
    return jax.shard_map(
        shards, mesh=mesh, in_specs=placed, out_specs=P("sketch", "demo"), check_vma=False
    )
```

```python
import math

import jax
import jax.numpy as jnp
from jax import lax
from jax.experimental import pallas as pl
from jax.experimental.pallas import tpu as pltpu
from jax.sharding import PartitionSpec as P

PROBE_ROWS = 64
PROBE_COLUMNS = 128
K = 8192
AXES = ("demo", "fsdp", "sketch")
Z, X, F, S = 8, 4, 2, 4
ROWS = 16
LEFT = 2 * PROBE_ROWS
RIGHT = 2 * PROBE_COLUMNS
LAST = ((1,), (1,))


def pairs(step):
    out = []
    for z in range(Z):
        for x in range(X):
            for f in range(F):
                for s in range(S):
                    z2, x2, f2, s2 = step(z, x, f, s)
                    source = ((z * X + x) * F + f) * S + s
                    target = (((z2 % Z) * X + x2 % X) * F + f2) * S + s2
                    out.append((source, target))
    return out


CORE = pairs(lambda z, x, f, s: (z, x, f, s ^ 1))
NEAR = pairs(lambda z, x, f, s: (z, x, f, s ^ 2))
CORE_NEAR = pairs(lambda z, x, f, s: (z, x, f, s ^ 3))
FAR = pairs(lambda z, x, f, s: (z, x, f ^ 1, s))
FAR_NEAR = pairs(lambda z, x, f, s: (z, x, f ^ 1, s ^ 2))


def shift(dz, dx):
    return pairs(lambda z, x, f, s: (z + dz, x + dx, f, s))


def send(value, moves):
    return lax.ppermute(value, AXES, moves)


def dot(a, b, contract):
    return lax.dot_general(a, b, (contract, ((), ())), preferred_element_type=jnp.float32)


def cost(flops, moved):
    return pl.CostEstimate(flops=flops, bytes_accessed=moved, transcendentals=0)


def shape(dims, kind=jnp.float32):
    return jax.ShapeDtypeStruct(dims, kind)


def weights_kernel(info_ref, contracting_ref, expanding_ref, queries_ref, weights_ref, squares_ref):
    columns = Z * X * ROWS
    column = lax.broadcasted_iota(jnp.int32, (1, columns), 1)
    kind = column % ROWS
    z_from = (info_ref[0] + Z - column // (X * ROWS)) % Z
    x_from = (info_ref[1] + X - (column // ROWS) % X) % X
    place = z_from * X + x_from

    def chosen(count, width, start):
        inside = (kind >= start) & (kind < start + width)
        target = jnp.where(inside, place * width + kind - start, -1)
        hit = lax.broadcasted_iota(jnp.int32, (count, columns), 0) == target
        return jnp.where(hit, 1.0, 0.0).astype(jnp.bfloat16)

    weights_ref[0:PROBE_ROWS] = chosen(PROBE_ROWS, 2, 12)
    weights_ref[PROBE_ROWS:LEFT] = dot(expanding_ref[...], chosen(128, 4, 0), ((1,), (0,))).astype(
        jnp.bfloat16
    )
    weights_ref[LEFT : LEFT + PROBE_COLUMNS] = dot(
        contracting_ref[...], chosen(128, 4, 4), ((0,), (0,))
    ).astype(jnp.bfloat16)
    weights_ref[LEFT + PROBE_COLUMNS :] = chosen(PROBE_COLUMNS, 4, 8)
    values = queries_ref[...].astype(jnp.float32)
    squares = jnp.sum(values * values, axis=1, keepdims=True)
    squares_ref[...] = jnp.broadcast_to(squares, (128, 128)).T[0:8]


def pick(value, index):
    return lax.dynamic_index_in_dim(value, index, 0, keepdims=False)


def shards(
    activations,
    cotangents,
    lengths,
    lowrank_contract_matrix,
    lowrank_expand_matrix,
    input_feature_sketch,
    latent_random_map_contracting,
    latent_random_map_expanding,
    output_feature_sketch,
    queries,
):
    demo_count, tok_local, feat = activations.shape
    own = demo_count // F
    tokens = demo_count * tok_local
    half = feat // 2
    nq = queries.shape[0]
    demo = lax.axis_index("demo")
    z, x = demo // X, demo % X
    f = lax.axis_index("fsdp")
    s = lax.axis_index("sketch")
    core = s % 2

    block = jnp.concatenate(
        [
            lowrank_contract_matrix.T,
            lowrank_expand_matrix.T,
            output_feature_sketch.T,
            input_feature_sketch.T,
            jnp.zeros((2, feat), jnp.bfloat16),
        ],
        axis=0,
    )
    block = lax.dynamic_slice_in_dim(block, core * half, half, axis=1)
    weights, query_squares = pl.pallas_call(
        weights_kernel,
        out_shape=[shape((LEFT + RIGHT, Z * X * ROWS), jnp.bfloat16), shape((8, 128))],
        in_specs=[pl.BlockSpec(memory_space=pltpu.SMEM)]
        + [pl.BlockSpec(memory_space=pltpu.VMEM)] * 3,
        out_specs=[pl.BlockSpec(memory_space=pltpu.VMEM)] * 2,
        cost_estimate=cost(10**8, 10**6),
    )(
        jnp.stack([z, x]).astype(jnp.int32),
        latent_random_map_contracting,
        latent_random_map_expanding.T,
        queries,
    )
    act = activations.reshape(tokens, feat)
    cot = cotangents.reshape(tokens, feat)

    def side(which):
        return jnp.stack(
            [lax.dynamic_slice_in_dim(v, which * half, half, axis=1) for v in (act, cot)]
        )

    line = jnp.concatenate([block] + [send(block, shift(0, k)) for k in range(1, X)])
    got = [line] + [None] * (Z - 1)
    up = down = line
    for k in range(1, Z // 2 + 1):
        up = send(up, shift(1, 0))
        got[k] = up
        if k < Z // 2:
            down = send(down, shift(-1, 0))
            got[Z - k] = down
        if k == 1:
            give = side(1 - core)
            give, up, down = lax.optimization_barrier((give, up, down))
            theirs = send(give, CORE)
        if k == 2:
            mine = side(core)
            mine, weights, query_squares, up, down = lax.optimization_barrier(
                (mine, weights, query_squares, up, down)
            )
        if k == 3:
            theirs, up, down = lax.optimization_barrier((theirs, up, down))
    rows = jnp.concatenate(got)
    maps = jnp.dot(weights, rows, preferred_element_type=jnp.float32).astype(jnp.bfloat16)
    left_map, right_map = maps[:LEFT], maps[LEFT:]

    right_away = send(dot(theirs[1], right_map, LAST), CORE)
    right = dot(mine[1], right_map, LAST) + right_away
    right = right.reshape(F, own, tok_local, RIGHT)
    right_sum = pick(right, f) + send(pick(right, 1 - f), FAR)
    left_away = send(dot(theirs[0], left_map, LAST), CORE)
    left = dot(mine[0], left_map, LAST) + left_away
    left = left.reshape(F, own, tok_local, LEFT)
    left_sum = pick(left, f) + send(pick(left, 1 - f), FAR)

    positions = s * tok_local + jnp.arange(tok_local, dtype=jnp.int32)
    own_lengths = pick(lengths.reshape(F, own), f)
    padding = (positions[None, :] < own_lengths[:, None]).astype(jnp.float32)
    right_sum = right_sum * padding[:, :, None]
    left_rows = left_sum.astype(jnp.bfloat16).reshape(own, tok_local, 2, PROBE_ROWS)
    right_rows = right_sum.astype(jnp.bfloat16).reshape(own, tok_local, 2, PROBE_COLUMNS)
    partial_value = jnp.einsum(
        "ntpa,ntpb->nab", left_rows, right_rows, preferred_element_type=jnp.float32
    )
    parts = partial_value.reshape(own, S, PROBE_ROWS // S, PROBE_COLUMNS)

    def part(k):
        return lax.dynamic_index_in_dim(parts, s ^ k, 1, keepdims=False)

    summed = (part(0) + send(part(1), CORE)) + (send(part(2), NEAR) + send(part(3), CORE_NEAR))
    demo_sketch = summed.astype(jnp.bfloat16).reshape(own, K // S)

    copies = jnp.broadcast_to(demo_sketch[None], (Z * X, own, K // S))
    every_demo = lax.all_to_all(copies, "demo", 0, 0).reshape(Z * X * own, K // S)
    inner = dot(every_demo, queries, LAST)
    every_f = every_demo.astype(jnp.float32)
    demo_squares = jnp.sum(every_f * every_f, axis=1, keepdims=True)
    both = jnp.concatenate([inner, jnp.broadcast_to(demo_squares, inner.shape)], axis=1)
    block_rows = Z * X * own // S
    both = both.reshape(S, block_rows, 2 * nq)
    extra = jnp.concatenate([query_squares, query_squares], axis=1)
    both = jnp.concatenate([both, jnp.broadcast_to(extra[None], (S, 8, 2 * nq))], axis=1)
    keep = jnp.stack([pick(both, s), pick(both, s ^ 2)])
    give = jnp.stack([pick(both, s ^ 1), pick(both, s ^ 3)])
    pair = keep + send(give, CORE)
    here = pair[0] + send(pair[1], NEAR)
    there = send(pair[0], FAR) + send(pair[1], FAR_NEAR)
    query_total = here[block_rows : block_rows + 1, :nq]
    here, there = here[:block_rows], there[:block_rows]
    total = jnp.stack([jnp.where(f == 0, here, there), jnp.where(f == 0, there, here)])
    total = total.reshape(F, block_rows // own, own, 2 * nq).transpose(1, 0, 2, 3)
    total = total.reshape(F * block_rows, 2 * nq)
    demo_norm = jnp.sqrt(total[:, nq:] + 1e-06)
    query_norm = jnp.sqrt(query_total + 1e-06)
    return math.sqrt(K) * total[:, :nq] / (demo_norm * query_norm)


def solution(mesh):
    placed = (
        P("demo", "sketch", "fsdp"),
        P("demo", "sketch", "fsdp"),
        P("demo"),
        P("fsdp", "demo"),
        P("fsdp", "demo"),
        P("fsdp", "demo"),
        P(),
        P(),
        P("fsdp", "demo"),
        P("demo", "sketch"),
    )
    return jax.shard_map(
        shards, mesh=mesh, in_specs=placed, out_specs=P("sketch", "demo"), check_vma=False
    )
```

```python
import math

import jax
import jax.numpy as jnp
from jax import lax
from jax.experimental import pallas as pl
from jax.experimental.pallas import tpu as pltpu
from jax.sharding import PartitionSpec as P

PROBE_ROWS = 64
PROBE_COLUMNS = 128
K = 8192
AXES = ("demo", "fsdp", "sketch")
Z, X, F, S = 8, 4, 2, 4
ROWS = 14
Z_BACK = (0, 1, 2, 6, 7, 3, 4, 5)
LEFT = 2 * PROBE_ROWS
RIGHT = 2 * PROBE_COLUMNS
LAST = ((1,), (1,))


def pairs(step):
    out = []
    for z in range(Z):
        for x in range(X):
            for f in range(F):
                for s in range(S):
                    z2, x2, f2, s2 = step(z, x, f, s)
                    source = ((z * X + x) * F + f) * S + s
                    target = (((z2 % Z) * X + x2 % X) * F + f2) * S + s2
                    out.append((source, target))
    return out


CORE = pairs(lambda z, x, f, s: (z, x, f, s ^ 1))
NEAR = pairs(lambda z, x, f, s: (z, x, f, s ^ 2))
CORE_NEAR = pairs(lambda z, x, f, s: (z, x, f, s ^ 3))
FAR = pairs(lambda z, x, f, s: (z, x, f ^ 1, s))
FAR_NEAR = pairs(lambda z, x, f, s: (z, x, f ^ 1, s ^ 2))


def shift(dz, dx):
    return pairs(lambda z, x, f, s: (z + dz, x + dx, f, s))


def send(value, moves):
    return lax.ppermute(value, AXES, moves)


def dot(a, b, contract):
    return lax.dot_general(a, b, (contract, ((), ())), preferred_element_type=jnp.float32)


def cost(flops, moved):
    return pl.CostEstimate(flops=flops, bytes_accessed=moved, transcendentals=0)


def shape(dims, kind=jnp.float32):
    return jax.ShapeDtypeStruct(dims, kind)


def weights_kernel(info_ref, contracting_ref, expanding_ref, queries_ref, weights_ref, squares_ref):
    columns = Z * X * ROWS
    column = lax.broadcasted_iota(jnp.int32, (1, columns), 1)
    block = jnp.zeros_like(column)
    for k in range(1, Z * X):
        block += jnp.where(column >= k * ROWS, 1, 0)
    kind = column - block * ROWS
    z_back = jnp.zeros_like(column)
    for k, back in enumerate(Z_BACK):
        z_back += jnp.where(block // X == k, back, 0)
    z_from = (info_ref[0] + Z - z_back) % Z
    x_from = (info_ref[1] + X - block % X) % X
    place = z_from * X + x_from

    def chosen(count, width, start):
        inside = (kind >= start) & (kind < start + width)
        target = jnp.where(inside, place * width + kind - start, -1)
        hit = lax.broadcasted_iota(jnp.int32, (count, columns), 0) == target
        return jnp.where(hit, 1.0, 0.0).astype(jnp.bfloat16)

    weights_ref[0:PROBE_ROWS] = chosen(PROBE_ROWS, 2, 12)
    weights_ref[PROBE_ROWS:LEFT] = dot(expanding_ref[...], chosen(128, 4, 0), ((1,), (0,))).astype(
        jnp.bfloat16
    )
    weights_ref[LEFT : LEFT + PROBE_COLUMNS] = dot(
        contracting_ref[...], chosen(128, 4, 4), ((0,), (0,))
    ).astype(jnp.bfloat16)
    weights_ref[LEFT + PROBE_COLUMNS :] = chosen(PROBE_COLUMNS, 4, 8)
    values = queries_ref[...].astype(jnp.float32)
    squares = jnp.sum(values * values, axis=1, keepdims=True)
    squares_ref[...] = jnp.broadcast_to(squares, (128, 128)).T[0:8]


def pick(value, index):
    return lax.dynamic_index_in_dim(value, index, 0, keepdims=False)


def shards(
    activations,
    cotangents,
    lengths,
    lowrank_contract_matrix,
    lowrank_expand_matrix,
    input_feature_sketch,
    latent_random_map_contracting,
    latent_random_map_expanding,
    output_feature_sketch,
    queries,
):
    demo_count, tok_local, feat = activations.shape
    own = demo_count // F
    tokens = demo_count * tok_local
    half = feat // 2
    nq = queries.shape[0]
    demo = lax.axis_index("demo")
    z, x = demo // X, demo % X
    f = lax.axis_index("fsdp")
    s = lax.axis_index("sketch")
    core = s % 2

    block = jnp.concatenate(
        [
            lax.dynamic_slice_in_dim(part.T, core * half, half, axis=1)
            for part in (
                lowrank_contract_matrix,
                lowrank_expand_matrix,
                output_feature_sketch,
                input_feature_sketch,
            )
        ]
    )
    weights, query_squares = pl.pallas_call(
        weights_kernel,
        out_shape=[shape((LEFT + RIGHT, Z * X * ROWS), jnp.bfloat16), shape((8, 128))],
        in_specs=[pl.BlockSpec(memory_space=pltpu.SMEM)]
        + [pl.BlockSpec(memory_space=pltpu.VMEM)] * 3,
        out_specs=[pl.BlockSpec(memory_space=pltpu.VMEM)] * 2,
        cost_estimate=cost(10**8, 10**6),
    )(
        jnp.stack([z, x]).astype(jnp.int32),
        latent_random_map_contracting,
        latent_random_map_expanding.T,
        queries,
    )
    line = jnp.concatenate([block] + [send(block, shift(0, k)) for k in range(1, X)])
    line, weights, query_squares = lax.optimization_barrier((line, weights, query_squares))
    up, down = [line], [line]
    for k in range(1, Z // 2 + 1):
        up.append(send(up[-1], shift(1, 0)))
        if k < Z // 2:
            down.append(send(down[-1], shift(-1, 0)))
        if k == 2:
            early = jnp.concatenate([up[0], up[1], up[2], down[2], down[1]])
            other_early = send(early, CORE)
    late = jnp.concatenate([up[3], up[4], down[3]])
    other_late = send(late, CORE)
    rows = jnp.concatenate([early, late])
    other = jnp.concatenate([other_early, other_late])
    maps = jnp.concatenate(
        [
            jnp.dot(
                weights, jnp.where(core == k, rows, other), preferred_element_type=jnp.float32
            ).astype(jnp.bfloat16)
            for k in (0, 1)
        ],
        axis=1,
    )
    left_map, right_map = maps[:LEFT], maps[LEFT:]
    right = dot(cotangents.reshape(tokens, feat), right_map, LAST)
    right = right.reshape(F, own, tok_local, RIGHT)
    give_right, left_map = lax.optimization_barrier((pick(right, 1 - f), left_map))
    right_sum = pick(right, f) + send(give_right, FAR)
    left = dot(activations.reshape(tokens, feat), left_map, LAST)
    left = left.reshape(F, own, tok_local, LEFT)
    left_sum = pick(left, f) + send(pick(left, 1 - f), FAR)

    positions = s * tok_local + jnp.arange(tok_local, dtype=jnp.int32)
    own_lengths = pick(lengths.reshape(F, own), f)
    padding = (positions[None, :] < own_lengths[:, None]).astype(jnp.float32)
    right_sum = right_sum * padding[:, :, None]
    left_rows = left_sum.astype(jnp.bfloat16).reshape(own, tok_local, 2, PROBE_ROWS)
    right_rows = right_sum.astype(jnp.bfloat16).reshape(own, tok_local, 2, PROBE_COLUMNS)
    partial_value = jnp.einsum(
        "ntpa,ntpb->nab", left_rows, right_rows, preferred_element_type=jnp.float32
    )
    parts = partial_value.reshape(own, S, PROBE_ROWS // S, PROBE_COLUMNS)

    def part(k):
        return lax.dynamic_index_in_dim(parts, s ^ k, 1, keepdims=False)

    summed = (part(0) + send(part(1), CORE)) + (send(part(2), NEAR) + send(part(3), CORE_NEAR))
    demo_sketch = summed.astype(jnp.bfloat16).reshape(own, K // S)

    copies = jnp.broadcast_to(demo_sketch[None], (Z * X, own, K // S))
    every_demo = lax.all_to_all(copies, "demo", 0, 0).reshape(Z * X * own, K // S)
    inner = dot(every_demo, queries, LAST)
    every_f = every_demo.astype(jnp.float32)
    demo_squares = jnp.sum(every_f * every_f, axis=1, keepdims=True)
    both = jnp.concatenate([inner, jnp.broadcast_to(demo_squares, inner.shape)], axis=1)
    block_rows = Z * X * own // S
    both = both.reshape(S, block_rows, 2 * nq)
    extra = jnp.concatenate([query_squares, query_squares], axis=1)
    both = jnp.concatenate([both, jnp.broadcast_to(extra[None], (S, 8, 2 * nq))], axis=1)
    keep = jnp.stack([pick(both, s), pick(both, s ^ 2)])
    give = jnp.stack([pick(both, s ^ 1), pick(both, s ^ 3)])
    pair = keep + send(give, CORE)
    here = pair[0] + send(pair[1], NEAR)
    there = send(pair[0], FAR) + send(pair[1], FAR_NEAR)
    query_total = here[block_rows : block_rows + 1, :nq]
    here, there = here[:block_rows], there[:block_rows]
    total = jnp.stack([jnp.where(f == 0, here, there), jnp.where(f == 0, there, here)])
    total = total.reshape(F, block_rows // own, own, 2 * nq).transpose(1, 0, 2, 3)
    total = total.reshape(F * block_rows, 2 * nq)
    demo_norm = jnp.sqrt(total[:, nq:] + 1e-06)
    query_norm = jnp.sqrt(query_total + 1e-06)
    return math.sqrt(K) * total[:, :nq] / (demo_norm * query_norm)


def solution(mesh):
    placed = (
        P("demo", "sketch", "fsdp"),
        P("demo", "sketch", "fsdp"),
        P("demo"),
        P("fsdp", "demo"),
        P("fsdp", "demo"),
        P("fsdp", "demo"),
        P(),
        P(),
        P("fsdp", "demo"),
        P("demo", "sketch"),
    )
    return jax.shard_map(
        shards, mesh=mesh, in_specs=placed, out_specs=P("sketch", "demo"), check_vma=False
    )
```

```python
import math

import jax
import jax.numpy as jnp
from jax import lax
from jax.experimental import pallas as pl
from jax.experimental.pallas import tpu as pltpu
from jax.sharding import PartitionSpec as P

PROBE_ROWS = 64
PROBE_COLUMNS = 128
K = 8192
AXES = ("demo", "fsdp", "sketch")
Z, X, F, S = 8, 4, 2, 4
ROWS = 14
Z_BACK = (0, 1, 2, 3, 5, 6, 7, 4)
LEFT = 2 * PROBE_ROWS
RIGHT = 2 * PROBE_COLUMNS
LAST = ((1,), (1,))


def pairs(step):
    out = []
    for z in range(Z):
        for x in range(X):
            for f in range(F):
                for s in range(S):
                    z2, x2, f2, s2 = step(z, x, f, s)
                    source = ((z * X + x) * F + f) * S + s
                    target = (((z2 % Z) * X + x2 % X) * F + f2) * S + s2
                    out.append((source, target))
    return out


CORE = pairs(lambda z, x, f, s: (z, x, f, s ^ 1))
NEAR = pairs(lambda z, x, f, s: (z, x, f, s ^ 2))
CORE_NEAR = pairs(lambda z, x, f, s: (z, x, f, s ^ 3))
FAR = pairs(lambda z, x, f, s: (z, x, f ^ 1, s))
FAR_NEAR = pairs(lambda z, x, f, s: (z, x, f ^ 1, s ^ 2))


def shift(dz, dx):
    return pairs(lambda z, x, f, s: (z + dz, x + dx, f, s))


def send(value, moves):
    return lax.ppermute(value, AXES, moves)


def dot(a, b, contract):
    return lax.dot_general(a, b, (contract, ((), ())), preferred_element_type=jnp.float32)


def cost(flops, moved):
    return pl.CostEstimate(flops=flops, bytes_accessed=moved, transcendentals=0)


def shape(dims, kind=jnp.float32):
    return jax.ShapeDtypeStruct(dims, kind)


def weights_kernel(info_ref, contracting_ref, expanding_ref, queries_ref, weights_ref, squares_ref):
    columns = Z * X * ROWS
    column = lax.broadcasted_iota(jnp.int32, (1, columns), 1)
    block = jnp.zeros_like(column)
    for k in range(1, Z * X):
        block += jnp.where(column >= k * ROWS, 1, 0)
    kind = column - block * ROWS
    z_back = jnp.zeros_like(column)
    for k, back in enumerate(Z_BACK):
        z_back += jnp.where(block // X == k, back, 0)
    z_from = (info_ref[0] + Z - z_back) % Z
    x_from = (info_ref[1] + X - block % X) % X
    place = z_from * X + x_from

    def chosen(count, width, start):
        inside = (kind >= start) & (kind < start + width)
        target = jnp.where(inside, place * width + kind - start, -1)
        hit = lax.broadcasted_iota(jnp.int32, (count, columns), 0) == target
        return jnp.where(hit, 1.0, 0.0).astype(jnp.bfloat16)

    weights_ref[0:PROBE_ROWS] = chosen(PROBE_ROWS, 2, 12)
    weights_ref[PROBE_ROWS:LEFT] = dot(expanding_ref[...], chosen(128, 4, 0), ((1,), (0,))).astype(
        jnp.bfloat16
    )
    weights_ref[LEFT : LEFT + PROBE_COLUMNS] = dot(
        contracting_ref[...], chosen(128, 4, 4), ((0,), (0,))
    ).astype(jnp.bfloat16)
    weights_ref[LEFT + PROBE_COLUMNS :] = chosen(PROBE_COLUMNS, 4, 8)
    values = queries_ref[...].astype(jnp.float32)
    squares = jnp.sum(values * values, axis=1, keepdims=True)
    squares_ref[...] = jnp.broadcast_to(squares, (128, 128)).T[0:8]


def pick(value, index):
    return lax.dynamic_index_in_dim(value, index, 0, keepdims=False)


def shards(
    activations,
    cotangents,
    lengths,
    lowrank_contract_matrix,
    lowrank_expand_matrix,
    input_feature_sketch,
    latent_random_map_contracting,
    latent_random_map_expanding,
    output_feature_sketch,
    queries,
):
    demo_count, tok_local, feat = activations.shape
    own = demo_count // F
    tokens = demo_count * tok_local
    half = feat // 2
    nq = queries.shape[0]
    demo = lax.axis_index("demo")
    z, x = demo // X, demo % X
    f = lax.axis_index("fsdp")
    s = lax.axis_index("sketch")
    core = s % 2

    block = jnp.concatenate(
        [
            lax.dynamic_slice_in_dim(part.T, core * half, half, axis=1)
            for part in (
                lowrank_contract_matrix,
                lowrank_expand_matrix,
                output_feature_sketch,
                input_feature_sketch,
            )
        ]
    )
    weights, query_squares = pl.pallas_call(
        weights_kernel,
        out_shape=[shape((LEFT + RIGHT, Z * X * ROWS), jnp.bfloat16), shape((8, 128))],
        in_specs=[pl.BlockSpec(memory_space=pltpu.SMEM)]
        + [pl.BlockSpec(memory_space=pltpu.VMEM)] * 3,
        out_specs=[pl.BlockSpec(memory_space=pltpu.VMEM)] * 2,
        cost_estimate=cost(10**8, 10**6),
    )(
        jnp.stack([z, x]).astype(jnp.int32),
        latent_random_map_contracting,
        latent_random_map_expanding.T,
        queries,
    )
    line = jnp.concatenate([block] + [send(block, shift(0, k)) for k in range(1, X)])
    line, weights, query_squares = lax.optimization_barrier((line, weights, query_squares))
    up, down = [line], [line]
    for k in range(1, Z // 2 + 1):
        up.append(send(up[-1], shift(1, 0)))
        if k < Z // 2:
            down.append(send(down[-1], shift(-1, 0)))
    early = jnp.concatenate(up[:4] + down[:0:-1])
    other_early = send(early, CORE)
    late = up[4]
    other_late = send(late, CORE)
    rows = jnp.concatenate([early, late])
    other = jnp.concatenate([other_early, other_late])
    maps = jnp.concatenate(
        [
            jnp.dot(
                weights, jnp.where(core == k, rows, other), preferred_element_type=jnp.float32
            ).astype(jnp.bfloat16)
            for k in (0, 1)
        ],
        axis=1,
    )
    left_map, right_map = maps[:LEFT], maps[LEFT:]
    right = dot(cotangents.reshape(tokens, feat), right_map, LAST)
    right = right.reshape(F, own, tok_local, RIGHT)
    right_sum = pick(right, f) + send(pick(right, 1 - f), FAR)
    left = dot(activations.reshape(tokens, feat), left_map, LAST)
    left = left.reshape(F, own, tok_local, LEFT)
    left_sum = pick(left, f) + send(pick(left, 1 - f), FAR)

    positions = s * tok_local + jnp.arange(tok_local, dtype=jnp.int32)
    own_lengths = pick(lengths.reshape(F, own), f)
    padding = (positions[None, :] < own_lengths[:, None]).astype(jnp.float32)
    right_sum = right_sum * padding[:, :, None]
    left_rows = left_sum.astype(jnp.bfloat16).reshape(own, tok_local, 2, PROBE_ROWS)
    right_rows = right_sum.astype(jnp.bfloat16).reshape(own, tok_local, 2, PROBE_COLUMNS)
    partial_value = jnp.einsum(
        "ntpa,ntpb->nab", left_rows, right_rows, preferred_element_type=jnp.float32
    )
    parts = partial_value.reshape(own, S, PROBE_ROWS // S, PROBE_COLUMNS)

    def part(k):
        return lax.dynamic_index_in_dim(parts, s ^ k, 1, keepdims=False)

    summed = (part(0) + send(part(1), CORE)) + (send(part(2), NEAR) + send(part(3), CORE_NEAR))
    demo_sketch = summed.astype(jnp.bfloat16).reshape(own, K // S)

    copies = jnp.broadcast_to(demo_sketch[None], (Z * X, own, K // S))
    every_demo = lax.all_to_all(copies, "demo", 0, 0).reshape(Z * X * own, K // S)
    inner = dot(every_demo, queries, LAST)
    every_f = every_demo.astype(jnp.float32)
    demo_squares = jnp.sum(every_f * every_f, axis=1, keepdims=True)
    both = jnp.concatenate([inner, jnp.broadcast_to(demo_squares, inner.shape)], axis=1)
    block_rows = Z * X * own // S
    both = both.reshape(S, block_rows, 2 * nq)
    extra = jnp.concatenate([query_squares, query_squares], axis=1)
    both = jnp.concatenate([both, jnp.broadcast_to(extra[None], (S, 8, 2 * nq))], axis=1)
    keep = jnp.stack([pick(both, s), pick(both, s ^ 2)])
    give = jnp.stack([pick(both, s ^ 1), pick(both, s ^ 3)])
    pair = keep + send(give, CORE)
    here = pair[0] + send(pair[1], NEAR)
    there = send(pair[0], FAR) + send(pair[1], FAR_NEAR)
    query_total = here[block_rows : block_rows + 1, :nq]
    here, there = here[:block_rows], there[:block_rows]
    total = jnp.stack([jnp.where(f == 0, here, there), jnp.where(f == 0, there, here)])
    total = total.reshape(F, block_rows // own, own, 2 * nq).transpose(1, 0, 2, 3)
    total = total.reshape(F * block_rows, 2 * nq)
    demo_norm = jnp.sqrt(total[:, nq:] + 1e-06)
    query_norm = jnp.sqrt(query_total + 1e-06)
    return math.sqrt(K) * total[:, :nq] / (demo_norm * query_norm)


def solution(mesh):
    placed = (
        P("demo", "sketch", "fsdp"),
        P("demo", "sketch", "fsdp"),
        P("demo"),
        P("fsdp", "demo"),
        P("fsdp", "demo"),
        P("fsdp", "demo"),
        P(),
        P(),
        P("fsdp", "demo"),
        P("demo", "sketch"),
    )
    return jax.shard_map(
        shards, mesh=mesh, in_specs=placed, out_specs=P("sketch", "demo"), check_vma=False
    )
```

```python
import math

import jax
import jax.numpy as jnp
from jax import lax
from jax.experimental import pallas as pl
from jax.experimental.pallas import tpu as pltpu
from jax.sharding import PartitionSpec as P

PROBE_ROWS = 64
PROBE_COLUMNS = 128
K = 8192
AXES = ("demo", "fsdp", "sketch")
Z, X, F, S = 8, 4, 2, 4
ROWS = 14
Z_BACK = (0, 1, 2, 6, 7, 3, 5, 4)
LEFT = 2 * PROBE_ROWS
RIGHT = 2 * PROBE_COLUMNS
LAST = ((1,), (1,))


def pairs(step):
    out = []
    for z in range(Z):
        for x in range(X):
            for f in range(F):
                for s in range(S):
                    z2, x2, f2, s2 = step(z, x, f, s)
                    source = ((z * X + x) * F + f) * S + s
                    target = (((z2 % Z) * X + x2 % X) * F + f2) * S + s2
                    out.append((source, target))
    return out


CORE = pairs(lambda z, x, f, s: (z, x, f, s ^ 1))
NEAR = pairs(lambda z, x, f, s: (z, x, f, s ^ 2))
CORE_NEAR = pairs(lambda z, x, f, s: (z, x, f, s ^ 3))
FAR = pairs(lambda z, x, f, s: (z, x, f ^ 1, s))


def shift(dz, dx):
    return pairs(lambda z, x, f, s: (z + dz, x + dx, f, s))


def send(value, moves):
    return lax.ppermute(value, AXES, moves)


def dot(a, b, contract):
    return lax.dot_general(a, b, (contract, ((), ())), preferred_element_type=jnp.float32)


def cost(flops, moved):
    return pl.CostEstimate(flops=flops, bytes_accessed=moved, transcendentals=0)


def shape(dims, kind=jnp.float32):
    return jax.ShapeDtypeStruct(dims, kind)


def weights_kernel(info_ref, contracting_ref, expanding_ref, queries_ref, weights_ref, squares_ref):
    columns = Z * X * ROWS
    column = lax.broadcasted_iota(jnp.int32, (1, columns), 1)
    block = jnp.zeros_like(column)
    for k in range(1, Z * X):
        block += jnp.where(column >= k * ROWS, 1, 0)
    kind = column - block * ROWS
    z_back = jnp.zeros_like(column)
    for k, back in enumerate(Z_BACK):
        z_back += jnp.where(block // X == k, back, 0)
    z_from = (info_ref[0] + Z - z_back) % Z
    x_from = (info_ref[1] + X - block % X) % X
    place = z_from * X + x_from

    def chosen(count, width, start):
        inside = (kind >= start) & (kind < start + width)
        target = jnp.where(inside, place * width + kind - start, -1)
        hit = lax.broadcasted_iota(jnp.int32, (count, columns), 0) == target
        return jnp.where(hit, 1.0, 0.0).astype(jnp.bfloat16)

    weights_ref[0:PROBE_ROWS] = chosen(PROBE_ROWS, 2, 12)
    weights_ref[PROBE_ROWS:LEFT] = dot(expanding_ref[...], chosen(128, 4, 0), ((1,), (0,))).astype(
        jnp.bfloat16
    )
    weights_ref[LEFT : LEFT + PROBE_COLUMNS] = dot(
        contracting_ref[...], chosen(128, 4, 4), ((0,), (0,))
    ).astype(jnp.bfloat16)
    weights_ref[LEFT + PROBE_COLUMNS :] = chosen(PROBE_COLUMNS, 4, 8)
    values = queries_ref[...].astype(jnp.float32)
    squares = jnp.sum(values * values, axis=1, keepdims=True)
    squares_ref[...] = jnp.broadcast_to(squares, (128, 128)).T[0:8]


def pick(value, index):
    return lax.dynamic_index_in_dim(value, index, 0, keepdims=False)


def shards(
    activations,
    cotangents,
    lengths,
    lowrank_contract_matrix,
    lowrank_expand_matrix,
    input_feature_sketch,
    latent_random_map_contracting,
    latent_random_map_expanding,
    output_feature_sketch,
    queries,
):
    demo_count, tok_local, feat = activations.shape
    own = demo_count // F
    tokens = demo_count * tok_local
    half = feat // 2
    nq = queries.shape[0]
    demo = lax.axis_index("demo")
    z, x = demo // X, demo % X
    f = lax.axis_index("fsdp")
    s = lax.axis_index("sketch")
    core = s % 2

    block = jnp.concatenate(
        [
            lax.dynamic_slice_in_dim(part.T, core * half, half, axis=1)
            for part in (
                lowrank_contract_matrix,
                lowrank_expand_matrix,
                output_feature_sketch,
                input_feature_sketch,
            )
        ]
    )
    weights, query_squares = pl.pallas_call(
        weights_kernel,
        out_shape=[shape((LEFT + RIGHT, Z * X * ROWS), jnp.bfloat16), shape((8, 128))],
        in_specs=[pl.BlockSpec(memory_space=pltpu.SMEM)]
        + [pl.BlockSpec(memory_space=pltpu.VMEM)] * 3,
        out_specs=[pl.BlockSpec(memory_space=pltpu.VMEM)] * 2,
        cost_estimate=cost(10**8, 10**6),
    )(
        jnp.stack([z, x]).astype(jnp.int32),
        latent_random_map_contracting,
        latent_random_map_expanding.T,
        queries,
    )
    line = jnp.concatenate([block] + [send(block, shift(0, k)) for k in range(1, X)])
    line, weights, query_squares = lax.optimization_barrier((line, weights, query_squares))
    up, down = [line], [line]
    for k in range(1, Z // 2):
        up.append(send(up[-1], shift(1, 0)))
        down.append(send(down[-1], shift(-1, 0)))
        if k == 2:
            early = jnp.concatenate([up[0], up[1], up[2], down[2], down[1]])
            other_early = send(early, CORE)
    cut = 32
    farthest = [send(up[3][:cut], shift(1, 0)), send(down[3][cut:], shift(-1, 0))]
    late = jnp.concatenate([up[3], down[3], *farthest])
    other_late = send(late, CORE)
    rows = jnp.concatenate([early, late])
    other = jnp.concatenate([other_early, other_late])
    maps = jnp.concatenate(
        [
            jnp.dot(
                weights, jnp.where(core == k, rows, other), preferred_element_type=jnp.float32
            ).astype(jnp.bfloat16)
            for k in (0, 1)
        ],
        axis=1,
    )
    left_map, right_map = maps[:LEFT], maps[LEFT:]
    right = dot(cotangents.reshape(tokens, feat), right_map, LAST)
    right = right.reshape(F, own, tok_local, RIGHT)
    right_sum = pick(right, f) + send(pick(right, 1 - f), FAR)
    left = dot(activations.reshape(tokens, feat), left_map, LAST)
    left = left.reshape(F, own, tok_local, LEFT)
    left_sum = pick(left, f) + send(pick(left, 1 - f), FAR)

    positions = s * tok_local + jnp.arange(tok_local, dtype=jnp.int32)
    own_lengths = pick(lengths.reshape(F, own), f)
    padding = (positions[None, :] < own_lengths[:, None]).astype(jnp.float32)
    right_sum = right_sum * padding[:, :, None]
    left_rows = left_sum.astype(jnp.bfloat16).reshape(own, tok_local, 2, PROBE_ROWS)
    right_rows = right_sum.astype(jnp.bfloat16).reshape(own, tok_local, 2, PROBE_COLUMNS)
    partial_value = jnp.einsum(
        "ntpa,ntpb->nab", left_rows, right_rows, preferred_element_type=jnp.float32
    )
    parts = partial_value.reshape(own, S, PROBE_ROWS // S, PROBE_COLUMNS)

    def part(k):
        return lax.dynamic_index_in_dim(parts, s ^ k, 1, keepdims=False)

    summed = (part(0) + send(part(1), CORE)) + (send(part(2), NEAR) + send(part(3), CORE_NEAR))
    demo_sketch = summed.astype(jnp.bfloat16).reshape(own, K // S)

    copies = jnp.broadcast_to(demo_sketch[None], (Z * X, own, K // S))
    every_demo = lax.all_to_all(copies, "demo", 0, 0).reshape(Z * X * own, K // S)
    inner = dot(every_demo, queries, LAST)
    every_f = every_demo.astype(jnp.float32)
    demo_squares = jnp.sum(every_f * every_f, axis=1, keepdims=True)
    both = jnp.concatenate([inner, jnp.broadcast_to(demo_squares, inner.shape)], axis=1)
    block_rows = Z * X * own // S
    both = both.reshape(S, block_rows, 2 * nq)
    extra = jnp.concatenate([query_squares, query_squares], axis=1)
    both = jnp.concatenate([both, jnp.broadcast_to(extra[None], (S, 8, 2 * nq))], axis=1)
    keep = jnp.stack([pick(both, s), pick(both, s ^ 2)])
    give = jnp.stack([pick(both, s ^ 1), pick(both, s ^ 3)])
    pair = keep + send(give, CORE)
    far = send(pair, FAR)
    wide = jnp.concatenate([pair, far[:, :block_rows]], axis=1)
    wide = wide[0] + send(wide[1], NEAR)
    query_total = wide[block_rows : block_rows + 1, :nq]
    here, there = wide[:block_rows], wide[block_rows + 8 :]
    total = jnp.stack([jnp.where(f == 0, here, there), jnp.where(f == 0, there, here)])
    total = total.reshape(F, block_rows // own, own, 2 * nq).transpose(1, 0, 2, 3)
    total = total.reshape(F * block_rows, 2 * nq)
    demo_norm = jnp.sqrt(total[:, nq:] + 1e-06)
    query_norm = jnp.sqrt(query_total + 1e-06)
    return math.sqrt(K) * total[:, :nq] / (demo_norm * query_norm)


def solution(mesh):
    placed = (
        P("demo", "sketch", "fsdp"),
        P("demo", "sketch", "fsdp"),
        P("demo"),
        P("fsdp", "demo"),
        P("fsdp", "demo"),
        P("fsdp", "demo"),
        P(),
        P(),
        P("fsdp", "demo"),
        P("demo", "sketch"),
    )
    return jax.shard_map(
        shards, mesh=mesh, in_specs=placed, out_specs=P("sketch", "demo"), check_vma=False
    )
```

```python
import math

import jax
import jax.numpy as jnp
from jax import lax
from jax.experimental import pallas as pl
from jax.experimental.pallas import tpu as pltpu
from jax.sharding import PartitionSpec as P

PROBE_ROWS = 64
PROBE_COLUMNS = 128
K = 8192
AXES = ("demo", "fsdp", "sketch")
Z, X, F, S = 8, 4, 2, 4
ROWS = 14
Z_BACK = (0, 1, 2, 6, 7, 3, 5, 4)
LEFT = 2 * PROBE_ROWS
RIGHT = 2 * PROBE_COLUMNS
LAST = ((1,), (1,))


def pairs(step):
    out = []
    for z in range(Z):
        for x in range(X):
            for f in range(F):
                for s in range(S):
                    z2, x2, f2, s2 = step(z, x, f, s)
                    source = ((z * X + x) * F + f) * S + s
                    target = (((z2 % Z) * X + x2 % X) * F + f2) * S + s2
                    out.append((source, target))
    return out


CORE = pairs(lambda z, x, f, s: (z, x, f, s ^ 1))
NEAR = pairs(lambda z, x, f, s: (z, x, f, s ^ 2))
CORE_NEAR = pairs(lambda z, x, f, s: (z, x, f, s ^ 3))
FAR = pairs(lambda z, x, f, s: (z, x, f ^ 1, s))
FAR_NEAR = pairs(lambda z, x, f, s: (z, x, f ^ 1, s ^ 2))


def shift(dz, dx):
    return pairs(lambda z, x, f, s: (z + dz, x + dx, f, s))


def send(value, moves):
    return lax.ppermute(value, AXES, moves)


def dot(a, b, contract):
    return lax.dot_general(a, b, (contract, ((), ())), preferred_element_type=jnp.float32)


def cost(flops, moved):
    return pl.CostEstimate(flops=flops, bytes_accessed=moved, transcendentals=0)


def shape(dims, kind=jnp.float32):
    return jax.ShapeDtypeStruct(dims, kind)


def weights_kernel(info_ref, contracting_ref, expanding_ref, queries_ref, weights_ref, squares_ref):
    columns = Z * X * ROWS
    column = lax.broadcasted_iota(jnp.int32, (1, columns), 1)
    block = jnp.zeros_like(column)
    for k in range(1, Z * X):
        block += jnp.where(column >= k * ROWS, 1, 0)
    kind = column - block * ROWS
    z_back = jnp.zeros_like(column)
    for k, back in enumerate(Z_BACK):
        z_back += jnp.where(block // X == k, back, 0)
    z_from = (info_ref[0] + Z - z_back) % Z
    x_from = (info_ref[1] + X - block % X) % X
    place = z_from * X + x_from

    def chosen(count, width, start):
        inside = (kind >= start) & (kind < start + width)
        target = jnp.where(inside, place * width + kind - start, -1)
        hit = lax.broadcasted_iota(jnp.int32, (count, columns), 0) == target
        return jnp.where(hit, 1.0, 0.0).astype(jnp.bfloat16)

    weights_ref[0:PROBE_ROWS] = chosen(PROBE_ROWS, 2, 12)
    weights_ref[PROBE_ROWS:LEFT] = dot(expanding_ref[...], chosen(128, 4, 0), ((1,), (0,))).astype(
        jnp.bfloat16
    )
    weights_ref[LEFT : LEFT + PROBE_COLUMNS] = dot(
        contracting_ref[...], chosen(128, 4, 4), ((0,), (0,))
    ).astype(jnp.bfloat16)
    weights_ref[LEFT + PROBE_COLUMNS :] = chosen(PROBE_COLUMNS, 4, 8)
    values = queries_ref[...].astype(jnp.float32)
    squares = jnp.sum(values * values, axis=1, keepdims=True)
    squares_ref[...] = jnp.broadcast_to(squares, (128, 128)).T[0:8]


def pick(value, index):
    return lax.dynamic_index_in_dim(value, index, 0, keepdims=False)


def shards(
    activations,
    cotangents,
    lengths,
    lowrank_contract_matrix,
    lowrank_expand_matrix,
    input_feature_sketch,
    latent_random_map_contracting,
    latent_random_map_expanding,
    output_feature_sketch,
    queries,
):
    demo_count, tok_local, feat = activations.shape
    own = demo_count // F
    tokens = demo_count * tok_local
    half = feat // 2
    nq = queries.shape[0]
    demo = lax.axis_index("demo")
    z, x = demo // X, demo % X
    f = lax.axis_index("fsdp")
    s = lax.axis_index("sketch")
    core = s % 2

    block = jnp.concatenate(
        [
            lax.dynamic_slice_in_dim(part.T, core * half, half, axis=1)
            for part in (
                lowrank_contract_matrix,
                lowrank_expand_matrix,
                output_feature_sketch,
                input_feature_sketch,
            )
        ]
    )
    weights, query_squares = pl.pallas_call(
        weights_kernel,
        out_shape=[shape((LEFT + RIGHT, Z * X * ROWS), jnp.bfloat16), shape((8, 128))],
        in_specs=[pl.BlockSpec(memory_space=pltpu.SMEM)]
        + [pl.BlockSpec(memory_space=pltpu.VMEM)] * 3,
        out_specs=[pl.BlockSpec(memory_space=pltpu.VMEM)] * 2,
        cost_estimate=cost(10**8, 10**6),
    )(
        jnp.stack([z, x]).astype(jnp.int32),
        latent_random_map_contracting,
        latent_random_map_expanding.T,
        queries,
    )
    line = jnp.concatenate([block] + [send(block, shift(0, k)) for k in range(1, X)])
    line, weights, query_squares = lax.optimization_barrier((line, weights, query_squares))
    up, down = [line], [line]
    for k in range(1, Z // 2):
        up.append(send(up[-1], shift(1, 0)))
        down.append(send(down[-1], shift(-1, 0)))
        if k == 2:
            early = jnp.concatenate([up[0], up[1], up[2], down[2], down[1]])
            other_early = send(early, CORE)
    cut = 32
    farthest = [send(up[3][:cut], shift(1, 0)), send(down[3][cut:], shift(-1, 0))]
    late = jnp.concatenate([up[3], down[3], *farthest])
    other_late = send(late, CORE)
    rows = jnp.concatenate([early, late])
    other = jnp.concatenate([other_early, other_late])
    sides = [jnp.where(core == k, rows, other) for k in (0, 1)]

    def build(part):
        return jnp.concatenate(
            [
                jnp.dot(part, side, preferred_element_type=jnp.float32).astype(jnp.bfloat16)
                for side in sides
            ],
            axis=1,
        )

    left_map, right_map = build(weights[:LEFT]), build(weights[LEFT:])
    cot = cotangents.reshape(F, tokens // F, feat)
    act = activations.reshape(F, tokens // F, feat)
    right_away = send(dot(pick(cot, 1 - f), right_map, LAST), FAR)
    left_away = send(dot(pick(act, 1 - f), left_map, LAST), FAR)
    right_here = dot(pick(cot, f), right_map, LAST)
    left_here = dot(pick(act, f), left_map, LAST)
    right_here, left_here = lax.optimization_barrier((right_here, left_here))
    right_sum = (right_here + right_away).reshape(own, tok_local, RIGHT)
    left_sum = (left_here + left_away).reshape(own, tok_local, LEFT)

    positions = s * tok_local + jnp.arange(tok_local, dtype=jnp.int32)
    own_lengths = pick(lengths.reshape(F, own), f)
    padding = (positions[None, :] < own_lengths[:, None]).astype(jnp.float32)
    right_sum = right_sum * padding[:, :, None]
    left_rows = left_sum.astype(jnp.bfloat16).reshape(own, tok_local, 2, PROBE_ROWS)
    right_rows = right_sum.astype(jnp.bfloat16).reshape(own, tok_local, 2, PROBE_COLUMNS)
    partial_value = jnp.einsum(
        "ntpa,ntpb->nab", left_rows, right_rows, preferred_element_type=jnp.float32
    )
    parts = partial_value.reshape(own, S, PROBE_ROWS // S, PROBE_COLUMNS)

    def part(k):
        return lax.dynamic_index_in_dim(parts, s ^ k, 1, keepdims=False)

    halves = jnp.stack([part(0), part(2)]) + send(jnp.stack([part(1), part(3)]), CORE)
    summed = halves[0] + send(halves[1], NEAR)
    demo_sketch = summed.astype(jnp.bfloat16).reshape(own, K // S)

    copies = jnp.broadcast_to(demo_sketch[None], (Z * X, own, K // S))
    every_demo = lax.all_to_all(copies, "demo", 0, 0).reshape(Z * X * own, K // S)
    inner = dot(every_demo, queries, LAST)
    every_f = every_demo.astype(jnp.float32)
    demo_squares = jnp.sum(every_f * every_f, axis=1, keepdims=True)
    both = jnp.concatenate([inner, jnp.broadcast_to(demo_squares, inner.shape)], axis=1)
    block_rows = Z * X * own // S
    both = both.reshape(S, block_rows, 2 * nq)
    extra = jnp.concatenate([query_squares, query_squares], axis=1)
    both = jnp.concatenate([both, jnp.broadcast_to(extra[None], (S, 8, 2 * nq))], axis=1)
    keep = jnp.stack([pick(both, s), pick(both, s ^ 2)])
    give = jnp.stack([pick(both, s ^ 1), pick(both, s ^ 3)])
    pair = keep + send(give, CORE)
    here = pair[0] + send(pair[1], NEAR)
    there = send(pair[0], FAR) + send(pair[1], FAR_NEAR)
    query_total = here[block_rows : block_rows + 1, :nq]
    here, there = here[:block_rows], there[:block_rows]
    total = jnp.stack([jnp.where(f == 0, here, there), jnp.where(f == 0, there, here)])
    total = total.reshape(F, block_rows // own, own, 2 * nq).transpose(1, 0, 2, 3)
    total = total.reshape(F * block_rows, 2 * nq)
    demo_norm = jnp.sqrt(total[:, nq:] + 1e-06)
    query_norm = jnp.sqrt(query_total + 1e-06)
    return math.sqrt(K) * total[:, :nq] / (demo_norm * query_norm)


def solution(mesh):
    placed = (
        P("demo", "sketch", "fsdp"),
        P("demo", "sketch", "fsdp"),
        P("demo"),
        P("fsdp", "demo"),
        P("fsdp", "demo"),
        P("fsdp", "demo"),
        P(),
        P(),
        P("fsdp", "demo"),
        P("demo", "sketch"),
    )
    return jax.shard_map(
        shards, mesh=mesh, in_specs=placed, out_specs=P("sketch", "demo"), check_vma=False
    )
```

```python
import math

import jax
import jax.numpy as jnp
from jax import lax
from jax.experimental import pallas as pl
from jax.experimental.pallas import tpu as pltpu
from jax.sharding import PartitionSpec as P

PROBE_ROWS = 64
PROBE_COLUMNS = 128
K = 8192
AXES = ("demo", "fsdp", "sketch")
Z, X, F, S = 8, 4, 2, 4
ROWS = 14
Z_BACK = (0, 1, 2, 6, 7, 3, 5, 4)
LEFT = 2 * PROBE_ROWS
RIGHT = 2 * PROBE_COLUMNS
LAST = ((1,), (1,))


def pairs(step):
    out = []
    for z in range(Z):
        for x in range(X):
            for f in range(F):
                for s in range(S):
                    z2, x2, f2, s2 = step(z, x, f, s)
                    source = ((z * X + x) * F + f) * S + s
                    target = (((z2 % Z) * X + x2 % X) * F + f2) * S + s2
                    out.append((source, target))
    return out


CORE = pairs(lambda z, x, f, s: (z, x, f, s ^ 1))
NEAR = pairs(lambda z, x, f, s: (z, x, f, s ^ 2))
CORE_NEAR = pairs(lambda z, x, f, s: (z, x, f, s ^ 3))
FAR = pairs(lambda z, x, f, s: (z, x, f ^ 1, s))
FAR_NEAR = pairs(lambda z, x, f, s: (z, x, f ^ 1, s ^ 2))


def shift(dz, dx):
    return pairs(lambda z, x, f, s: (z + dz, x + dx, f, s))


def send(value, moves):
    return lax.ppermute(value, AXES, moves)


def dot(a, b, contract):
    return lax.dot_general(a, b, (contract, ((), ())), preferred_element_type=jnp.float32)


def cost(flops, moved):
    return pl.CostEstimate(flops=flops, bytes_accessed=moved, transcendentals=0)


def shape(dims, kind=jnp.float32):
    return jax.ShapeDtypeStruct(dims, kind)


def weights_kernel(info_ref, contracting_ref, expanding_ref, queries_ref, weights_ref, squares_ref):
    columns = Z * X * ROWS
    column = lax.broadcasted_iota(jnp.int32, (1, columns), 1)
    block = jnp.zeros_like(column)
    for k in range(1, Z * X):
        block += jnp.where(column >= k * ROWS, 1, 0)
    kind = column - block * ROWS
    z_back = jnp.zeros_like(column)
    for k, back in enumerate(Z_BACK):
        z_back += jnp.where(block // X == k, back, 0)
    z_from = (info_ref[0] + Z - z_back) % Z
    x_from = (info_ref[1] + X - block % X) % X
    place = z_from * X + x_from

    def chosen(count, width, start):
        inside = (kind >= start) & (kind < start + width)
        target = jnp.where(inside, place * width + kind - start, -1)
        hit = lax.broadcasted_iota(jnp.int32, (count, columns), 0) == target
        return jnp.where(hit, 1.0, 0.0).astype(jnp.bfloat16)

    weights_ref[0:PROBE_ROWS] = chosen(PROBE_ROWS, 2, 12)
    weights_ref[PROBE_ROWS:LEFT] = dot(expanding_ref[...], chosen(128, 4, 0), ((1,), (0,))).astype(
        jnp.bfloat16
    )
    weights_ref[LEFT : LEFT + PROBE_COLUMNS] = dot(
        contracting_ref[...], chosen(128, 4, 4), ((0,), (0,))
    ).astype(jnp.bfloat16)
    weights_ref[LEFT + PROBE_COLUMNS :] = chosen(PROBE_COLUMNS, 4, 8)
    values = queries_ref[...].astype(jnp.float32)
    squares = jnp.sum(values * values, axis=1, keepdims=True)
    squares_ref[...] = jnp.broadcast_to(squares, (128, 128)).T[0:8]


def pick(value, index):
    return lax.dynamic_index_in_dim(value, index, 0, keepdims=False)


def shards(
    activations,
    cotangents,
    lengths,
    lowrank_contract_matrix,
    lowrank_expand_matrix,
    input_feature_sketch,
    latent_random_map_contracting,
    latent_random_map_expanding,
    output_feature_sketch,
    queries,
):
    demo_count, tok_local, feat = activations.shape
    own = demo_count // F
    tokens = demo_count * tok_local
    half = feat // 2
    nq = queries.shape[0]
    demo = lax.axis_index("demo")
    z, x = demo // X, demo % X
    f = lax.axis_index("fsdp")
    s = lax.axis_index("sketch")
    core = s % 2

    block, start = None, 0
    for part in (
        lowrank_contract_matrix,
        lowrank_expand_matrix,
        output_feature_sketch,
        input_feature_sketch,
    ):
        rows = lax.dynamic_slice_in_dim(part.T, core * half, half, axis=1)
        rows = jnp.pad(rows, ((start, ROWS - start - rows.shape[0]), (0, 0)))
        block = rows if block is None else block + rows
        start += part.shape[1]
    weights, query_squares = pl.pallas_call(
        weights_kernel,
        out_shape=[shape((LEFT + RIGHT, Z * X * ROWS), jnp.bfloat16), shape((8, 128))],
        in_specs=[pl.BlockSpec(memory_space=pltpu.SMEM)]
        + [pl.BlockSpec(memory_space=pltpu.VMEM)] * 3,
        out_specs=[pl.BlockSpec(memory_space=pltpu.VMEM)] * 2,
        cost_estimate=cost(10**8, 10**6),
    )(
        jnp.stack([z, x]).astype(jnp.int32),
        latent_random_map_contracting,
        latent_random_map_expanding.T,
        queries,
    )
    line = jnp.concatenate([block] + [send(block, shift(0, k)) for k in range(1, X)])
    line, weights, query_squares = lax.optimization_barrier((line, weights, query_squares))
    up, down = [line], [line]
    for k in range(1, Z // 2):
        up.append(send(up[-1], shift(1, 0)))
        down.append(send(down[-1], shift(-1, 0)))
        if k == 2:
            early = jnp.concatenate([up[0], up[1], up[2], down[2], down[1]])
            other_early = send(early, CORE)
    cut = 32
    farthest = [send(up[3][:cut], shift(1, 0)), send(down[3][cut:], shift(-1, 0))]
    late = jnp.concatenate([up[3], down[3], *farthest])
    other_late = send(late, CORE)
    rows = jnp.concatenate([early, late])
    other = jnp.concatenate([other_early, other_late])
    sides = [jnp.where(core == k, rows, other) for k in (0, 1)]

    def build(part):
        return jnp.concatenate(
            [
                jnp.dot(part, side, preferred_element_type=jnp.float32).astype(jnp.bfloat16)
                for side in sides
            ],
            axis=1,
        )

    left_map, right_map = build(weights[:LEFT]), build(weights[LEFT:])
    cot = cotangents.reshape(F, tokens // F, feat)
    act = activations.reshape(F, tokens // F, feat)
    right_away = send(dot(pick(cot, 1 - f), right_map, LAST), FAR)
    left_away = send(dot(pick(act, 1 - f), left_map, LAST), FAR)
    right_here = dot(pick(cot, f), right_map, LAST)
    left_here = dot(pick(act, f), left_map, LAST)
    right_here, left_here = lax.optimization_barrier((right_here, left_here))
    right_sum = (right_here + right_away).reshape(own, tok_local, RIGHT)
    left_sum = (left_here + left_away).reshape(own, tok_local, LEFT)

    positions = s * tok_local + jnp.arange(tok_local, dtype=jnp.int32)
    own_lengths = pick(lengths.reshape(F, own), f)
    padding = (positions[None, :] < own_lengths[:, None]).astype(jnp.float32)
    right_sum = right_sum * padding[:, :, None]
    left_rows = left_sum.astype(jnp.bfloat16).reshape(own, tok_local, 2, PROBE_ROWS)
    right_rows = right_sum.astype(jnp.bfloat16).reshape(own, tok_local, 2, PROBE_COLUMNS)
    partial_value = jnp.einsum(
        "ntpa,ntpb->nab", left_rows, right_rows, preferred_element_type=jnp.float32
    )
    parts = partial_value.reshape(own, S, PROBE_ROWS // S, PROBE_COLUMNS)

    def part(k):
        return lax.dynamic_index_in_dim(parts, s ^ k, 1, keepdims=False)

    halves = jnp.stack([part(0), part(2)]) + send(jnp.stack([part(1), part(3)]), CORE)
    summed = halves[0] + send(halves[1], NEAR)
    demo_sketch = summed.astype(jnp.bfloat16).reshape(own, K // S)

    copies = jnp.broadcast_to(demo_sketch[None], (Z * X, own, K // S))
    every_demo = lax.all_to_all(copies, "demo", 0, 0).reshape(Z * X * own, K // S)
    inner = dot(every_demo, queries, LAST)
    every_f = every_demo.astype(jnp.float32)
    demo_squares = jnp.sum(every_f * every_f, axis=1, keepdims=True)
    both = inner
    block_rows = Z * X * own // S
    spread = jnp.broadcast_to(demo_squares, inner.shape).reshape(S, block_rows, nq)
    both = both.reshape(S, block_rows, nq)
    extra = jnp.broadcast_to(query_squares[None], (S, 8, nq))
    both = jnp.concatenate([both, spread, extra], axis=1)
    keep = jnp.stack([pick(both, s), pick(both, s ^ 2)])
    give = jnp.stack([pick(both, s ^ 1), pick(both, s ^ 3)])
    pair = keep + send(give, CORE)
    here = pair[0] + send(pair[1], NEAR)
    there = send(pair[0], FAR) + send(pair[1], FAR_NEAR)
    query_total = here[2 * block_rows : 2 * block_rows + 1]
    total = jnp.stack([jnp.where(f == 0, here, there), jnp.where(f == 0, there, here)])
    total = total[:, : 2 * block_rows].reshape(F, 2, block_rows // own, own, nq)
    total = total.transpose(1, 2, 0, 3, 4).reshape(2, F * block_rows, nq)
    demo_norm = jnp.sqrt(total[1] + 1e-06)
    query_norm = jnp.sqrt(query_total + 1e-06)
    return math.sqrt(K) * total[0] / (demo_norm * query_norm)


def solution(mesh):
    placed = (
        P("demo", "sketch", "fsdp"),
        P("demo", "sketch", "fsdp"),
        P("demo"),
        P("fsdp", "demo"),
        P("fsdp", "demo"),
        P("fsdp", "demo"),
        P(),
        P(),
        P("fsdp", "demo"),
        P("demo", "sketch"),
    )
    return jax.shard_map(
        shards, mesh=mesh, in_specs=placed, out_specs=P("sketch", "demo"), check_vma=False
    )
```
